32 devices in a mesh: expert: 8 (over z, y), hidden: 4 (over x, core).
Axes of the slice: x: 2, y: 2, z: 4, core: 2. Of those that a mesh axis runs over, the one named last changes fastest.
Arguments:
- tokens: bfloat16 [512, 7168], P('expert'), may hold values from -6 to 6
- expert_ids: int32 [512, 8], replicated, may hold values from 0 to 31, all different within a row; in each aligned block of 64 rows (0 to 63, 64 to 127, ...) at most 24 rows name the same one
- gate_weight: bfloat16 [32, 7168, 2048], P('expert', None, 'hidden')
- up_weight: bfloat16 [32, 7168, 2048], P('expert', None, 'hidden')
Outputs:
- expert_hidden: bfloat16 [32, 8, 24, 2048], P('expert', None, None, 'hidden')
The draws below stay inside these ranges and needn't reach their ends.
Inputs may be any that keep to these rules, and one draw needn't show every extreme that they name: `expert_ids`: each row names 8 different experts; among the rows of one device no expert is named more than 24 times, and in every draw some expert is named exactly 24 times there.
All inputs are finite; a program needn't handle non-finite values.
Results may differ from the reference program's by a relative error of at most 0.0058.
Values may be sent and summed in bfloat16 or wider, within the bound.
A program may use at most 192 MiB of HBM per device.

```python
import math
import jax
import jax.numpy as jnp
import numpy as np
from jax import lax

D = 7168
FF = 2048
TOPK = 8
EXPERTS = 32
SWEEPS = 5
TOK_DEV = 64
CAP = 24
TOKENS = 512


def row_places(key):
    shared = jax.random.fold_in(key, 7)
    spread = jax.random.uniform(shared, (EXPERTS, D, 1), jnp.float32, 0.0, 1.0)
    return 8.0 * spread * spread


def weight_common(key, salt, reverse):
    places = row_places(key)
    key = jax.random.fold_in(key, salt)
    keys = jax.random.split(key, 5)
    base = jax.random.normal(keys[0], (EXPERTS, D, FF), jnp.float32)
    row_part = jnp.exp(jax.random.uniform(keys[1], (EXPERTS, D, 1), jnp.float32, 0.0, math.log(10.0)))
    col_part = jnp.exp(jax.random.uniform(keys[2], (EXPERTS, 1, FF), jnp.float32, 0.0, math.log(4.0)))
    rough = jnp.exp(math.log(16.0) * (jax.random.uniform(keys[3], (EXPERTS, D, FF), jnp.float32, 0.0, 1.0) - 0.5))
    block = (jnp.arange(FF, dtype=jnp.int32) // (FF // 4)).astype(jnp.float32)
    if reverse:
        block = 3.0 - block
    within = jax.random.uniform(keys[4], (EXPERTS, 1, FF), jnp.float32, 0.0, 1.0)
    col_places = 2.0 * block[None, None, :] + 2.0 * within
    band = jnp.exp(-1.2 * jnp.abs(places - col_places))
    values = base * row_part * col_part * rough * band / math.sqrt(D)
    return values.astype(jnp.bfloat16)


def draw_gate_weight(key, part):
    return weight_common(key, 11, False)


def draw_up_weight(key, part):
    return weight_common(key, 23, True)


def level_of(key, shape, cuts, least, top_value):
    def one(axis_at, shards_of):
        heights = jax.random.uniform(jax.random.fold_in(jax.random.fold_in(key, 6), axis_at), (shards_of,), jnp.float32, least / len(cuts), top_value / len(cuts))
        return jnp.repeat(jnp.exp(heights), shape[axis_at] // shards_of).reshape((-1,) + (1,) * (len(shape) - axis_at - 1))

    gain = one(*cuts[0])
    for cut in cuts[1:]:
        gain = gain * one(*cut)
    return gain


def deal_out(stream_key, own, number, rows, count, top, most, skew):
    order = jax.random.permutation(stream_key, count)
    heavy_load, ordinary = load_shares(count, rows * top, most, skew, True), load_shares(count, rows * top, most, skew, False)
    places = jnp.arange(count)

    def named(tallies, rotation):
        used = int((tallies > 0).sum())
        fixed = max(1, used // 4)
        passed = fixed + (places - fixed + rotation * (used - fixed)) % max(1, count - fixed)
        return jnp.zeros((count,), jnp.int32).at[order[jnp.where(places < fixed, places, passed)]].set(jnp.asarray(tallies, jnp.int32))

    tallies = jnp.where(number % 4 == 0, named(heavy_load, number // 4), named(ordinary, number - number // 4 - 1))
    mixed = jax.random.permutation(jax.random.fold_in(own, 3), count)
    donor, receiver = mixed[0:count // 2 * 2:2], mixed[1:count // 2 * 2:2]
    room = jnp.minimum(tallies[donor] - 1, most - tallies[receiver]) // 2
    room = jnp.where((donor == order[0]) | (receiver == order[0]) | (tallies[receiver] == 0), 0, jnp.maximum(room, 0))
    passed = jax.random.randint(jax.random.fold_in(own, 4), (count // 2,), 0, 1 << 20) % (room + 1)
    tallies = tallies.at[donor].add(-passed).at[receiver].add(passed)
    members = jnp.searchsorted(jnp.cumsum(tallies), jnp.arange(rows * top), side="right").astype(jnp.int32)
    table = members.reshape(top, rows).T
    table = table[jax.random.permutation(jax.random.fold_in(own, 1), rows)]
    rotation = jax.random.randint(jax.random.fold_in(own, 2), (rows, 1), 0, top)
    return jnp.take_along_axis(table, (jnp.arange(top)[None, :] + rotation) % top, axis=1)


def load_shares(amount, total, bound, lean, full):
    loads = [(1 << 20) // math.isqrt(standing ** lean) + 1 for standing in range(1, amount + 1)]
    largest = bound if full else min(bound, max(-(-total // amount), total * loads[0] // sum(loads)))
    least = 1 if total - largest >= amount - 1 else 0
    counts, rest = [largest] + [least] * (amount - 1), total - largest - least * (amount - 1)
    while rest > 0:
        free = [i for i in range(1, amount) if counts[i] < largest] or [i for i in range(1, amount) if counts[i] < bound]
        mass, remaining = sum([loads[i] for i in free]), rest
        for i in free:
            extra = min(bound - counts[i], max(1, remaining * loads[i] // mass), rest)
            counts[i] = counts[i] + extra
            rest = rest - extra
    return np.array(counts)


def scatter_about(own_key, dims, deviation, most, cuts=(), held_as=jnp.bfloat16):
    loudness = level_of(own_key, dims, cuts, -0.22, 0.18) if cuts else 1.0
    array = jax.random.normal(own_key, dims, jnp.float32) * deviation * loudness
    return jnp.minimum(jnp.maximum(array, -most), most).astype(held_as)


def setup_inputs(seed: int = 0) -> dict:
    splits = jax.random.split(jax.random.key(seed), 5)
    tokens = scatter_about(splits[0], (TOKENS, D), 1.0, 6.0, ((0, 8),))
    expert_ids_keys = jax.random.split(jax.random.fold_in(splits[1], 1), TOKENS // TOK_DEV)
    expert_ids_turns = jax.random.permutation(jax.random.fold_in(splits[1], 3), TOKENS // TOK_DEV)
    expert_ids = jax.vmap(lambda own, number: deal_out(jax.random.fold_in(splits[1], 2), own, number, TOK_DEV, EXPERTS, TOPK, CAP, 2))(expert_ids_keys, expert_ids_turns).reshape((TOKENS, TOPK))
    gate_weight = draw_gate_weight(jax.random.fold_in(splits[4], 71), 0)
    up_weight = draw_up_weight(jax.random.fold_in(splits[4], 71), 0)
    return {"tokens": tokens, "expert_ids": expert_ids, "gate_weight": gate_weight, "up_weight": up_weight}


EPS = 1e-06

def slot_table(block_ids):
    flat_ids = block_ids.reshape(-1)
    onehot = (flat_ids[:, None] == jnp.arange(EXPERTS, dtype=jnp.int32)[None, :]).astype(jnp.int32)
    before = jnp.cumsum(onehot, axis=0) - onehot
    my_rank = lax.optimization_barrier(jnp.sum(before * onehot, axis=1))
    token_index = (jnp.arange(flat_ids.shape[0], dtype=jnp.int32) // TOPK).astype(jnp.int32)
    position = flat_ids * CAP + my_rank
    filled = jnp.full((EXPERTS * CAP,), TOK_DEV, jnp.int32).at[position].set(token_index)
    return filled.reshape(EXPERTS, CAP)

def equilibrate(gate_w, up_w):
    gate_f = gate_w.astype(jnp.float32)
    up_f = up_w.astype(jnp.float32)
    gate_sq = gate_f * gate_f
    up_sq = up_f * up_f
    gate_cols = jnp.ones((FF,), jnp.float32)
    up_cols = jnp.ones((FF,), jnp.float32)
    high = lax.Precision.HIGHEST
    for sweep in range(SWEEPS):
        row_sums = jnp.dot(gate_sq, gate_cols * gate_cols, precision=high) + jnp.dot(up_sq, up_cols * up_cols, precision=high)
        row_scale = lax.rsqrt(D * row_sums / (2 * FF) + EPS)
        gate_cols = lax.rsqrt(jnp.dot(row_scale * row_scale, gate_sq, precision=high) + EPS)
        up_cols = lax.rsqrt(jnp.dot(row_scale * row_scale, up_sq, precision=high) + EPS)
    gate_eq = (gate_f * row_scale[:, None] * gate_cols[None, :]).astype(jnp.bfloat16)
    up_eq = (up_f * row_scale[:, None] * up_cols[None, :]).astype(jnp.bfloat16)
    return (gate_eq, up_eq)

def reference(tokens, expert_ids, gate_weight, up_weight):
    sources = TOKENS // TOK_DEV
    tables = jax.vmap(slot_table)(expert_ids.reshape(sources, TOK_DEV, TOPK))
    offsets = (jnp.arange(sources, dtype=jnp.int32) * TOK_DEV)[:, None, None]
    global_index = jnp.where(tables == TOK_DEV, TOKENS, tables + offsets).astype(jnp.int32)
    global_index = jnp.transpose(global_index, (1, 0, 2))
    padded = jnp.concatenate([tokens, jnp.zeros((1, D), jnp.bfloat16)], axis=0)

    def one_expert(operands):
        gate_w, up_w, index_block = operands
        gate_eq, up_eq = equilibrate(gate_w, up_w)
        gathered = padded[index_block.reshape(-1)]
        gate_act = jnp.dot(gathered, gate_eq, preferred_element_type=jnp.float32)
        up_act = jnp.dot(gathered, up_eq, preferred_element_type=jnp.float32)
        result = (jax.nn.silu(gate_act) * up_act).astype(jnp.bfloat16)
        return result.reshape(sources, CAP, FF)
    return lax.map(one_expert, (gate_weight, up_weight, global_index))
```

```python
import functools

import jax
import jax.numpy as jnp
from jax import lax
from jax.experimental import pallas as pl
from jax.experimental.pallas import tpu as pltpu
from jax.sharding import PartitionSpec as P

TOPK = 8
EXPERTS = 32
SWEEPS = 5
CAP = 24
EPS = 1e-06

F32 = jnp.float32
BF16 = jnp.bfloat16
NT = (((1,), (1,)), ((), ()))
BLOCK = 1792


def sweep_kernel(
    peers, gate_hbm, up_hbm, scale_ref, cols_ref, gate, up, mine, theirs, load_sem, send_sem, recv_sem
):
    experts, width, ff = gate.shape
    block = BLOCK if width % BLOCK == 0 else width
    blocks = width // block
    total_ff = ff * peers
    me = lax.axis_index("hidden")

    def load(e, i):
        src, dst = ((gate_hbm, gate), (up_hbm, up))[i]
        return pltpu.make_async_copy(src.at[e], dst.at[e], load_sem.at[e, i])

    for e in range(experts):
        load(e, 0).start()
        load(e, 1).start()

    barrier = pltpu.get_barrier_semaphore()
    for j in range(1, peers):
        pl.semaphore_signal(
            barrier,
            inc=1,
            device_id={"hidden": lax.rem(me + j, peers)},
            device_id_type=pl.DeviceIdType.MESH,
        )
    pl.semaphore_wait(barrier, peers - 1)

    def send(slot, e, j):
        return pltpu.make_async_remote_copy(
            src_ref=mine.at[slot, e],
            dst_ref=theirs.at[slot, e, j - 1],
            send_sem=send_sem.at[slot, e, j - 1],
            recv_sem=recv_sem.at[slot, e, j - 1],
            device_id={"hidden": lax.rem(me + j, peers)},
            device_id_type=pl.DeviceIdType.MESH,
        )

    ones = jnp.ones((16, 128), BF16)

    def rows(slot, e):
        gate_sq = cols_ref[e, 0] * cols_ref[e, 0]
        up_sq = cols_ref[e, 1] * cols_ref[e, 1]
        gate_sq, up_sq = gate_sq.astype(BF16), up_sq.astype(BF16)

        @pl.loop(0, blocks)
        def _(b):
            span = pl.ds(pl.multiple_of(b * block, block), block)
            parts = []
            for ref, cols in ((gate, gate_sq), (up, up_sq)):
                w = ref[e, span, :]
                w = w * w * cols
                parts += [w[:, i : i + 128] for i in range(0, ff, 128)]
            while len(parts) > 1:
                parts = [
                    parts[i] + parts[i + 1] if i + 1 < len(parts) else parts[i]
                    for i in range(0, len(parts), 2)
                ]
            sums = lax.dot_general(ones, parts[0], NT, preferred_element_type=F32)
            mine[slot, e, :, span] = sums[0:1]

        for j in range(1, peers):
            send(slot, e, j).start()

    def columns(slot, e):
        for j in range(1, peers):
            send(slot, e, j).wait()
        sums = mine[slot, e]
        for j in range(1, peers):
            sums = sums + theirs[slot, e, j - 1]
        scale = lax.rsqrt(width * sums / (2 * total_ff) + EPS)
        scale_ref[e] = scale

        def body(b, acc):
            span = pl.ds(pl.multiple_of(b * block, block), block)
            s = scale_ref[e, :, span]
            sq = jnp.broadcast_to(s * s, (16, block))
            high = sq.astype(BF16).astype(F32)
            row = lax.broadcasted_iota(jnp.int32, (16, block), 0)
            lhs = jnp.where(row == 0, high, jnp.where(row == 1, sq - high, 0.0)).astype(BF16)
            out = []
            for ref, total in ((gate, acc[0]), (up, acc[1])):
                w = ref[e, span, :]
                out.append(total + jnp.dot(lhs, w * w, preferred_element_type=F32))
            return tuple(out)

        zero = jnp.zeros((16, ff), F32)
        for i, total in enumerate(lax.fori_loop(0, blocks, body, (zero, zero))):
            cols_ref[e, i] = lax.rsqrt(total[0:1] + total[1:2] + EPS)

    cols_ref[...] = jnp.ones_like(cols_ref)

    @pl.loop(0, experts)
    def _(e):
        load(e, 0).wait()
        load(e, 1).wait()
        rows(0, e)

    @pl.loop(0, (SWEEPS - 1) * experts)
    def _(step):
        e = lax.rem(step, experts)
        slot = lax.rem(step // experts, 2)
        columns(slot, e)
        rows(1 - slot, e)

    @pl.loop(0, experts)
    def _(e):
        columns((SWEEPS - 1) % 2, e)


def sweeps(gate_weight, up_weight):
    experts, width, ff = gate_weight.shape
    peers = lax.axis_size("hidden")
    return pl.pallas_call(
        functools.partial(sweep_kernel, peers),
        out_shape=(
            jax.ShapeDtypeStruct((experts, 1, width), F32),
            jax.ShapeDtypeStruct((experts, 2, 1, ff), F32),
        ),
        in_specs=[pl.BlockSpec(memory_space=pltpu.HBM)] * 2,
        out_specs=(pl.BlockSpec(memory_space=pltpu.VMEM),) * 2,
        scratch_shapes=[
            pltpu.VMEM((experts, width, ff), BF16),
            pltpu.VMEM((experts, width, ff), BF16),
            pltpu.VMEM((2, experts, 1, width), F32),
            pltpu.VMEM((2, experts, peers - 1, 1, width), F32),
            pltpu.SemaphoreType.DMA((experts, 2)),
            pltpu.SemaphoreType.DMA((2, experts, peers - 1)),
            pltpu.SemaphoreType.DMA((2, experts, peers - 1)),
        ],
        compiler_params=pltpu.CompilerParams(
            collective_id=0, has_side_effects=True, vmem_limit_bytes=(64 << 20) - (256 << 10)
        ),
        cost_estimate=pl.CostEstimate(
            flops=4 * 10 * experts * width * ff,
            bytes_accessed=20 * experts * width * ff,
            transcendentals=0,
        ),
    )(gate_weight, up_weight)


def act_kernel(pick_ref, tokens_ref, scale_ref, cols_ref, gate_ref, up_ref, out_ref, acc):
    b, e = pl.program_id(0), pl.program_id(1)
    x = jnp.dot(pick_ref[e], tokens_ref[...], preferred_element_type=F32)
    x = (x * scale_ref[e]).astype(BF16)
    gate = jnp.dot(x, gate_ref[0], preferred_element_type=F32)
    up = jnp.dot(x, up_ref[0], preferred_element_type=F32)

    @pl.when(b == 0)
    def _():
        acc[e, 0] = gate
        acc[e, 1] = up

    @pl.when(b > 0)
    def _():
        acc[e, 0] += gate
        acc[e, 1] += up

    @pl.when(b == pl.num_programs(0) - 1)
    def _():
        g = acc[e, 0] * cols_ref[e, 0]
        u = acc[e, 1] * cols_ref[e, 1]
        out_ref[e] = (g / (1.0 + jnp.exp(-g)) * u).astype(BF16)


def activations(pick, tokens, scale, cols, gate_weight, up_weight):
    experts, width, ff = gate_weight.shape
    count, slots = tokens.shape[0], pick.shape[1]
    block = 1024 if width % 1024 == 0 else width
    whole = pl.BlockSpec(memory_space=pltpu.VMEM)
    weight = pl.BlockSpec((1, block, ff), lambda b, e: (e, b, 0))
    return pl.pallas_call(
        act_kernel,
        grid=(width // block, experts),
        out_shape=jax.ShapeDtypeStruct((experts, slots, ff), BF16),
        in_specs=[
            whole,
            pl.BlockSpec((count, block), lambda b, e: (0, b)),
            pl.BlockSpec((experts, 1, block), lambda b, e: (0, 0, b)),
            whole,
            weight,
            weight,
        ],
        out_specs=whole,
        scratch_shapes=[pltpu.VMEM((experts, 2, slots, ff), F32)],
        compiler_params=pltpu.CompilerParams(vmem_limit_bytes=48 << 20),
        cost_estimate=pl.CostEstimate(
            flops=4 * experts * slots * width * ff,
            bytes_accessed=4 * experts * width * ff,
            transcendentals=0,
        ),
    )(pick, tokens, scale, cols, gate_weight, up_weight)


def pick_table(expert_ids, first, experts, tok_local):
    sources = expert_ids.shape[0] // tok_local
    wanted = first + jnp.arange(experts, dtype=jnp.int32)
    named = jnp.any(expert_ids[None] == wanted[:, None, None], axis=2)
    named = named.reshape(experts, sources, tok_local)
    lower = jnp.arange(tok_local)[:, None] < jnp.arange(tok_local)[None, :]
    rank = jnp.dot(named.astype(BF16), lower.astype(BF16), preferred_element_type=F32)
    slot = jnp.where(named, rank.astype(jnp.int32), -1)
    slot = slot + jnp.arange(sources, dtype=jnp.int32)[None, :, None] * CAP
    slot = jnp.where(named, slot, -1).reshape(experts, 1, sources * tok_local)
    places = jnp.arange(sources * CAP, dtype=jnp.int32)[None, :, None]
    return (slot == places).astype(BF16)


def shards(tokens, expert_ids, gate_weight, up_weight):
    experts, width, ff = gate_weight.shape
    tok_local = tokens.shape[0]
    sources = lax.axis_size("expert")
    everyone = lax.all_gather(tokens, "expert", axis=0, tiled=True)
    scale, cols = sweeps(gate_weight, up_weight)
    pick = pick_table(expert_ids, lax.axis_index("expert") * experts, experts, tok_local)
    out = activations(pick, everyone, scale, cols, gate_weight, up_weight)
    return out.reshape(experts, sources, CAP, ff)


def solution(mesh):
    in_specs = (P("expert", None), P(), P("expert", None, "hidden"), P("expert", None, "hidden"))
    out_specs = P("expert", None, None, "hidden")
    return jax.shard_map(shards, mesh=mesh, in_specs=in_specs, out_specs=out_specs, check_vma=False)
```

```python
import functools

import jax
import jax.numpy as jnp
from jax import lax
from jax.experimental import pallas as pl
from jax.experimental.pallas import tpu as pltpu
from jax.sharding import PartitionSpec as P

TOPK = 8
EXPERTS = 32
SWEEPS = 5
CAP = 24
EPS = 1e-06

F32 = jnp.float32
BF16 = jnp.bfloat16
NT = (((1,), (1,)), ((), ()))
BLOCK = 3584


def sweep_kernel(
    peers, gate_hbm, up_hbm, scale_ref, cols_ref, gate, up, mine, theirs, load_sem, send_sem, recv_sem
):
    experts, width, ff = gate.shape
    block = BLOCK if width % BLOCK == 0 else width
    blocks = width // block
    total_ff = ff * peers
    me = lax.axis_index("hidden")

    def load(e, i):
        src, dst = ((gate_hbm, gate), (up_hbm, up))[i]
        return pltpu.make_async_copy(src.at[e], dst.at[e], load_sem.at[e, i])

    for e in range(experts):
        load(e, 0).start()
        load(e, 1).start()

    barrier = pltpu.get_barrier_semaphore()
    for j in range(1, peers):
        pl.semaphore_signal(
            barrier,
            inc=1,
            device_id={"hidden": lax.rem(me + j, peers)},
            device_id_type=pl.DeviceIdType.MESH,
        )
    pl.semaphore_wait(barrier, peers - 1)

    def send(slot, e, j):
        return pltpu.make_async_remote_copy(
            src_ref=mine.at[slot, e],
            dst_ref=theirs.at[slot, e, j - 1],
            send_sem=send_sem.at[slot, e, j - 1],
            recv_sem=recv_sem.at[slot, e, j - 1],
            device_id={"hidden": lax.rem(me + j, peers)},
            device_id_type=pl.DeviceIdType.MESH,
        )

    ones = jnp.ones((16, 128), BF16)

    def rows(slot, e):
        gate_sq = cols_ref[e, 0] * cols_ref[e, 0]
        up_sq = cols_ref[e, 1] * cols_ref[e, 1]
        gate_sq, up_sq = gate_sq.astype(BF16), up_sq.astype(BF16)

        @pl.loop(0, blocks)
        def _(b):
            span = pl.ds(pl.multiple_of(b * block, block), block)
            parts = []
            for ref, cols in ((gate, gate_sq), (up, up_sq)):
                w = ref[e, span, :]
                w = w * w * cols
                parts += [w[:, i : i + 128] for i in range(0, ff, 128)]
            while len(parts) > 1:
                parts = [
                    parts[i] + parts[i + 1] if i + 1 < len(parts) else parts[i]
                    for i in range(0, len(parts), 2)
                ]
            sums = lax.dot_general(ones, parts[0], NT, preferred_element_type=F32)
            mine[slot, e, :, span] = sums[0:1]

        for j in range(1, peers):
            send(slot, e, j).start()

    def columns(slot, e):
        for j in range(1, peers):
            send(slot, e, j).wait()
        sums = mine[slot, e]
        for j in range(1, peers):
            sums = sums + theirs[slot, e, j - 1]
        scale = lax.rsqrt(width * sums / (2 * total_ff) + EPS)
        scale_ref[e] = scale

        def body(b, acc):
            span = pl.ds(pl.multiple_of(b * block, block), block)
            s = scale_ref[e, :, span]
            sq = jnp.broadcast_to(s * s, (16, block))
            high = sq.astype(BF16).astype(F32)
            row = lax.broadcasted_iota(jnp.int32, (16, block), 0)
            lhs = jnp.where(row == 0, high, jnp.where(row == 1, sq - high, 0.0)).astype(BF16)
            out = []
            for ref, total in ((gate, acc[0]), (up, acc[1])):
                w = ref[e, span, :]
                out.append(total + jnp.dot(lhs, w * w, preferred_element_type=F32))
            return tuple(out)

        zero = jnp.zeros((16, ff), F32)
        for i, total in enumerate(lax.fori_loop(0, blocks, body, (zero, zero))):
            cols_ref[e, i] = lax.rsqrt(total[0:1] + total[1:2] + EPS)

    cols_ref[...] = jnp.ones_like(cols_ref)

    @pl.loop(0, experts)
    def _(e):
        load(e, 0).wait()
        load(e, 1).wait()
        rows(0, e)

    @pl.loop(0, (SWEEPS - 1) * experts)
    def _(step):
        e = lax.rem(step, experts)
        slot = lax.rem(step // experts, 2)
        columns(slot, e)
        rows(1 - slot, e)

    @pl.loop(0, experts)
    def _(e):
        columns((SWEEPS - 1) % 2, e)


def sweeps(gate_weight, up_weight):
    experts, width, ff = gate_weight.shape
    peers = lax.axis_size("hidden")
    return pl.pallas_call(
        functools.partial(sweep_kernel, peers),
        out_shape=(
            jax.ShapeDtypeStruct((experts, 1, width), F32),
            jax.ShapeDtypeStruct((experts, 2, 1, ff), F32),
        ),
        in_specs=[pl.BlockSpec(memory_space=pltpu.HBM)] * 2,
        out_specs=(pl.BlockSpec(memory_space=pltpu.VMEM),) * 2,
        scratch_shapes=[
            pltpu.VMEM((experts, width, ff), BF16),
            pltpu.VMEM((experts, width, ff), BF16),
            pltpu.VMEM((2, experts, 1, width), F32),
            pltpu.VMEM((2, experts, peers - 1, 1, width), F32),
            pltpu.SemaphoreType.DMA((experts, 2)),
            pltpu.SemaphoreType.DMA((2, experts, peers - 1)),
            pltpu.SemaphoreType.DMA((2, experts, peers - 1)),
        ],
        compiler_params=pltpu.CompilerParams(
            collective_id=0, has_side_effects=True, vmem_limit_bytes=(64 << 20) - (256 << 10)
        ),
        cost_estimate=pl.CostEstimate(
            flops=4 * 10 * experts * width * ff,
            bytes_accessed=20 * experts * width * ff,
            transcendentals=0,
        ),
    )(gate_weight, up_weight)


def act_kernel(pick_ref, tokens_ref, scale_ref, cols_ref, gate_ref, up_ref, out_ref, acc):
    b, e = pl.program_id(0), pl.program_id(1)
    x = jnp.dot(pick_ref[e], tokens_ref[...], preferred_element_type=F32)
    x = (x * scale_ref[e]).astype(BF16)
    gate = jnp.dot(x, gate_ref[0], preferred_element_type=F32)
    up = jnp.dot(x, up_ref[0], preferred_element_type=F32)

    @pl.when(b == 0)
    def _():
        acc[e, 0] = gate
        acc[e, 1] = up

    @pl.when(b > 0)
    def _():
        acc[e, 0] += gate
        acc[e, 1] += up

    @pl.when(b == pl.num_programs(0) - 1)
    def _():
        g = acc[e, 0] * cols_ref[e, 0]
        u = acc[e, 1] * cols_ref[e, 1]
        out_ref[e] = (g / (1.0 + jnp.exp(-g)) * u).astype(BF16)


def activations(pick, tokens, scale, cols, gate_weight, up_weight):
    experts, width, ff = gate_weight.shape
    count, slots = tokens.shape[0], pick.shape[1]
    block = 1792 if width % 1792 == 0 else width
    whole = pl.BlockSpec(memory_space=pltpu.VMEM)
    weight = pl.BlockSpec((1, block, ff), lambda b, e: (e, b, 0))
    return pl.pallas_call(
        act_kernel,
        grid=(width // block, experts),
        out_shape=jax.ShapeDtypeStruct((experts, slots, ff), BF16),
        in_specs=[
            whole,
            pl.BlockSpec((count, block), lambda b, e: (0, b)),
            pl.BlockSpec((experts, 1, block), lambda b, e: (0, 0, b)),
            whole,
            weight,
            weight,
        ],
        out_specs=whole,
        scratch_shapes=[pltpu.VMEM((experts, 2, slots, ff), F32)],
        compiler_params=pltpu.CompilerParams(vmem_limit_bytes=48 << 20),
        cost_estimate=pl.CostEstimate(
            flops=4 * experts * slots * width * ff,
            bytes_accessed=4 * experts * width * ff,
            transcendentals=0,
        ),
    )(pick, tokens, scale, cols, gate_weight, up_weight)


def pick_table(expert_ids, first, experts, tok_local):
    sources = expert_ids.shape[0] // tok_local
    wanted = first + jnp.arange(experts, dtype=jnp.int32)
    named = jnp.any(expert_ids[None] == wanted[:, None, None], axis=2)
    named = named.reshape(experts, sources, tok_local)
    lower = jnp.arange(tok_local)[:, None] < jnp.arange(tok_local)[None, :]
    rank = jnp.dot(named.astype(BF16), lower.astype(BF16), preferred_element_type=F32)
    slot = jnp.where(named, rank.astype(jnp.int32), -1)
    slot = slot + jnp.arange(sources, dtype=jnp.int32)[None, :, None] * CAP
    slot = jnp.where(named, slot, -1).reshape(experts, 1, sources * tok_local)
    places = jnp.arange(sources * CAP, dtype=jnp.int32)[None, :, None]
    return (slot == places).astype(BF16)


def shards(tokens, expert_ids, gate_weight, up_weight):
    experts, width, ff = gate_weight.shape
    tok_local = tokens.shape[0]
    sources = lax.axis_size("expert")
    everyone = lax.all_gather(tokens, "expert", axis=0, tiled=True)
    scale, cols = sweeps(gate_weight, up_weight)
    pick = pick_table(expert_ids, lax.axis_index("expert") * experts, experts, tok_local)
    out = activations(pick, everyone, scale, cols, gate_weight, up_weight)
    return out.reshape(experts, sources, CAP, ff)


def solution(mesh):
    in_specs = (P("expert", None), P(), P("expert", None, "hidden"), P("expert", None, "hidden"))
    out_specs = P("expert", None, None, "hidden")
    return jax.shard_map(shards, mesh=mesh, in_specs=in_specs, out_specs=out_specs, check_vma=False)
```
